32 devices in a mesh: sky: 16 (over z, x, core), exp: 2 (over y).
Axes of the slice: x: 2, y: 2, z: 4, core: 2. Of those that a mesh axis runs over, the one named last changes fastest.
Arguments:
- padded_tiles: bfloat16 [1536, 10752], P(('sky', 'exp')), may hold values from -6 to 6
- coefficients: float32 [1536, 20], P(('sky', 'exp')), may hold values from -1.8 to 1.8
- row_taps: bfloat16 [1536, 6, 24], P(('sky', 'exp')), may hold values from 0.019897461 to 0.34960938
- col_taps: bfloat16 [1536, 6, 128], P(('sky', 'exp')), may hold values from 0.019897461 to 0.34960938
- shifts: int32 [1536, 2], P(('sky', 'exp')), may hold values from 0 to 2
- mask_words: int32 [1536], P(('sky', 'exp')), may hold values from -2147483648 to 2147483646
- weights: bfloat16 [1536], P(('sky', 'exp')), may hold values from 0.049804688 to 0.5
- destination: int32 [1536, 1], P(('sky', 'exp')), may hold values from 0 to 15; in each aligned block of 48 rows (0 to 47, 48 to 95, ...) at most 6 rows name the same one
- patch_slot: int32 [1536], P(('sky', 'exp')), may hold values from 0 to 15
- basis_rows: bfloat16 [20, 41], replicated, may hold values from -1 to 1
- basis_cols: bfloat16 [20, 41], replicated, may hold values from -1 to 1
Outputs:
- coadd: float32 [6144, 128], P(('sky', 'exp'))
The draws below stay inside these ranges and needn't reach their ends.
Inputs may be any that keep to these rules, and one draw needn't show every extreme that they name: `destination`: the 48 tiles of one device name one patch at most 6 times, a bound that some block reaches.
All inputs are finite; a program needn't handle non-finite values.
Results may differ from the reference program's by a relative error of at most 0.014.
Values may be sent and summed in bfloat16 or wider, within the bound.
A program may use at most 64 MiB of HBM per device.

```python
import math
import jax
import jax.numpy as jnp
import numpy as np
from jax import lax

NB = 20
KW = 41
TR = 24
TC = 128
BW = 6
SLOTS = 16
TILES_DEV = 48
CAP = 6
TILES = 1536
N_SKY = 16
N_EXP = 2


def set_ends(values, own_key, smallest, largest):
    longest = values.shape.index(max(values.shape))
    spots = []
    for shift in (0, 1):
        where = [jax.random.randint(jax.random.fold_in(own_key, axis), (), 0, length) for axis, length in enumerate(values.shape)]
        where[longest] = (where[longest] + shift) % values.shape[longest]
        spots.append(tuple(where))
    return values.at[spots[0]].set(smallest).at[spots[1]].set(largest)


def shard_levels(rng, dims, split, smallest, largest):
    loudness, own = 1.0, jax.random.fold_in(rng, 6)
    for position, blocks in split:
        heights = jnp.exp(jax.random.uniform(jax.random.fold_in(own, position), (blocks,), jnp.float32, smallest / len(split), largest / len(split)))
        loudness = loudness * jnp.repeat(heights, dims[position] // blocks).reshape([-1 if axis == position else 1 for axis in range(len(dims))])
    return loudness


def deal_out(key, own, number, rows, number_of, top, bound, lean):
    order = jax.random.permutation(key, number_of)
    crowded, usual = shares(number_of, rows * top, bound, lean, True), shares(number_of, rows * top, bound, lean, False)
    places = jnp.arange(number_of)

    def named(sizes, turn):
        used = int((sizes > 0).sum())
        fixed = max(1, used // 4)
        shifted = fixed + (places - fixed + turn * (used - fixed)) % max(1, number_of - fixed)
        return jnp.zeros((number_of,), jnp.int32).at[order[jnp.where(places < fixed, places, shifted)]].set(jnp.asarray(sizes, jnp.int32))

    sizes = jnp.where(number % 4 == 0, named(crowded, number // 4), named(usual, number - number // 4 - 1))
    mixed = jax.random.permutation(jax.random.fold_in(own, 3), number_of)
    donor, sink = mixed[0:number_of // 2 * 2:2], mixed[1:number_of // 2 * 2:2]
    room = jnp.minimum(sizes[donor] - 1, bound - sizes[sink]) // 2
    room = jnp.where((donor == order[0]) | (sink == order[0]) | (sizes[sink] == 0), 0, jnp.maximum(room, 0))
    shifted = jax.random.randint(jax.random.fold_in(own, 4), (number_of // 2,), 0, 1 << 20) % (room + 1)
    sizes = sizes.at[donor].add(-shifted).at[sink].add(shifted)
    items = jnp.searchsorted(jnp.cumsum(sizes), jnp.arange(rows * top), side="right").astype(jnp.int32)
    listing = items.reshape(top, rows).T
    listing = listing[jax.random.permutation(jax.random.fold_in(own, 1), rows)]
    turn = jax.random.randint(jax.random.fold_in(own, 2), (rows, 1), 0, top)
    return jnp.take_along_axis(listing, (jnp.arange(top)[None, :] + turn) % top, axis=1)


def shares(count, total, limit, skew, full):
    loads = [(1 << 20) // math.isqrt(standing ** skew) + 1 for standing in range(1, count + 1)]
    largest = limit if full else min(limit, max(-(-total // count), total * loads[0] // sum(loads)))
    least = 1 if total - largest >= count - 1 else 0
    given, rest = [largest] + [least] * (count - 1), total - largest - least * (count - 1)
    while rest > 0:
        movable = [i for i in range(1, count) if given[i] < largest] or [i for i in range(1, count) if given[i] < limit]
        pool, budget = sum([loads[i] for i in movable]), rest
        for i in movable:
            extra = min(limit - given[i], max(1, budget * loads[i] // pool), rest)
            given[i] = given[i] + extra
            rest = rest - extra
    return np.array(given)


def noise(own_key, extent, spread, bound, shards=(), kind=jnp.bfloat16):
    level = shard_levels(own_key, extent, shards, -0.22, 0.18) if shards else 1.0
    result = jax.random.normal(own_key, extent, jnp.float32) * spread * level
    return jnp.minimum(jnp.maximum(result, -bound), bound).astype(kind)


def setup_inputs(seed: int = 0) -> dict:
    streams_of = jax.random.split(jax.random.key(seed), 12)
    padded_tiles = noise(streams_of[0], (TILES, (TR + KW - 1) * (TC + KW - 1)), 1.0, 6.0, ((0, 32),))
    coefficients = noise(streams_of[1], (TILES, NB), 0.3, 1.8, ((0, 32),), jnp.float32)
    row_taps = jnp.clip(0.019897461 + 0.3297119 * jax.random.uniform(streams_of[2], (TILES, BW, TR), jnp.float32) ** shard_levels(streams_of[2], (TILES, BW, TR), ((0, 32),), -0.2, 0.2), 0.019897461, 0.34960938).astype(jnp.bfloat16)
    col_taps = jnp.clip(0.019897461 + 0.3297119 * jax.random.uniform(streams_of[3], (TILES, BW, TC), jnp.float32) ** shard_levels(streams_of[3], (TILES, BW, TC), ((0, 32),), -0.2, 0.2), 0.019897461, 0.34960938).astype(jnp.bfloat16)
    shifts = set_ends(jax.random.randint(streams_of[4], (TILES, 2), 0, 3), jax.random.fold_in(streams_of[4], 1), 0, 2).astype(jnp.int32)
    mask_words = set_ends(jax.random.randint(streams_of[5], (TILES,), -2147483648, 2147483647), jax.random.fold_in(streams_of[5], 1), -2147483648, 2147483646).astype(jnp.int32)
    weights = jnp.clip(jnp.exp(math.log(0.5) - 2.306499 * jax.random.uniform(streams_of[6], (TILES,), jnp.float32) ** shard_levels(streams_of[6], (TILES,), ((0, 32),), -0.2, 0.2)), 0.049804688, 0.5).astype(jnp.bfloat16)
    destination_keys = jax.random.split(jax.random.fold_in(streams_of[7], 1), TILES // TILES_DEV)
    destination_turns = jax.random.permutation(jax.random.fold_in(streams_of[7], 3), TILES // TILES_DEV)
    destination = jax.vmap(lambda own, number: deal_out(jax.random.fold_in(streams_of[7], 2), own, number, TILES_DEV, N_SKY, 1, CAP, 2))(destination_keys, destination_turns).reshape((TILES, 1))
    patch_slot = set_ends(jax.random.randint(streams_of[8], (TILES,), 0, SLOTS), jax.random.fold_in(streams_of[8], 1), 0, SLOTS - 1).astype(jnp.int32)
    basis_rows = noise(streams_of[9], (NB, KW), KW ** -0.5, 1.0)
    basis_cols = noise(streams_of[10], (NB, KW), KW ** -0.5, 1.0)
    return {"padded_tiles": padded_tiles, "coefficients": coefficients, "row_taps": row_taps, "col_taps": col_taps, "shifts": shifts, "mask_words": mask_words, "weights": weights, "destination": destination, "patch_slot": patch_slot, "basis_rows": basis_rows, "basis_cols": basis_cols}


def toeplitz(basis_vals, distance):
    kernel_len = basis_vals.shape[1]
    picks = (distance[:, :, None] == jnp.arange(kernel_len, dtype=jnp.int32)[None, None, :]).astype(jnp.float32)
    return jnp.einsum('xyk,bk->bxy', picks, basis_vals.astype(jnp.float32)).astype(jnp.bfloat16)


def build_tables(basis_rows, basis_cols, tile_rows, tile_cols):
    kernel_len = basis_rows.shape[1]
    out_rows = jnp.arange(tile_rows, dtype=jnp.int32)
    in_rows = jnp.arange(tile_rows + kernel_len - 1, dtype=jnp.int32)
    out_cols = jnp.arange(tile_cols, dtype=jnp.int32)
    in_cols = jnp.arange(tile_cols + kernel_len - 1, dtype=jnp.int32)
    row_toeplitz = toeplitz(basis_rows, in_rows[None, :] - out_rows[:, None])
    col_toeplitz = toeplitz(basis_cols, in_cols[:, None] - out_cols[None, :])
    return row_toeplitz, col_toeplitz


def band_matrix(tap_values, band_shift):
    tap_count = tap_values.shape[1]
    length = tap_values.shape[2]
    positions = jnp.arange(length, dtype=jnp.int32)
    band_start = jnp.clip(positions[None, :] + band_shift[:, None] - tap_count // 2, 0, length - tap_count)
    band_offset = positions[None, None, :] - band_start[:, :, None]
    matrix = jnp.zeros((tap_values.shape[0], length, length), tap_values.dtype)
    for tap_index in range(tap_count):
        matrix = matrix + jnp.where(band_offset == tap_index, tap_values[:, tap_index, :][:, :, None], jnp.zeros((), tap_values.dtype))
    return matrix


def mask_good(mask_words, tile_rows, tile_cols):
    bit_index = jnp.arange(32, dtype=jnp.int32)
    flagged = jnp.bitwise_and(jnp.right_shift(mask_words[:, None], bit_index[None, :]), 1)
    good_cells = (1 - flagged).astype(jnp.float32).reshape(mask_words.shape[0], 4, 8)
    good_cells = jnp.repeat(good_cells, tile_rows // 4, axis=1)
    return jnp.repeat(good_cells, tile_cols // 8, axis=2)


def match_and_warp(padded, coefficients, row_taps, col_taps, shifts, row_toeplitz, col_toeplitz):
    row_pass = jnp.einsum('bic,ncj->nbij', row_toeplitz.astype(jnp.float32), padded.astype(jnp.float32))
    scaled = (row_pass * coefficients[:, :, None, None]).astype(jnp.bfloat16)
    matched = jnp.einsum('nbij,bjk->nik', scaled.astype(jnp.float32), col_toeplitz.astype(jnp.float32)).astype(jnp.bfloat16)
    row_warp = band_matrix(row_taps, shifts[:, 0])
    col_warp = band_matrix(col_taps, shifts[:, 1])
    halfway = jnp.einsum('nij,njk->nik', row_warp.astype(jnp.float32), matched.astype(jnp.float32)).astype(jnp.bfloat16)
    return jnp.einsum('nij,nkj->nik', halfway.astype(jnp.float32), col_warp.astype(jnp.float32)).astype(jnp.bfloat16)


def reference(padded_tiles, coefficients, row_taps, col_taps, shifts, mask_words, weights, destination, patch_slot, basis_rows, basis_cols):
    row_toeplitz, col_toeplitz = build_tables(basis_rows, basis_cols, TR, TC)
    block_count = N_SKY * N_EXP
    inputs = (padded_tiles, coefficients, row_taps, col_taps, shifts, mask_words, weights, destination, patch_slot)
    grouped = tuple(arr.reshape((block_count, TILES_DEV) + arr.shape[1:]) for arr in inputs)

    def accumulate(state_pair, tile_group):
        numerator, weight_sum = state_pair
        padded, coef_block, rtap, ctap, shift_block, words, weight_block, dest_block, slot_block = tile_group
        padded = padded.reshape(TILES_DEV, TR + KW - 1, TC + KW - 1)
        warped = match_and_warp(padded, coef_block, rtap, ctap, shift_block, row_toeplitz, col_toeplitz)
        good_cells = mask_good(words, TR, TC)
        weight_plane = (weight_block.astype(jnp.float32)[:, None, None] * good_cells).astype(jnp.bfloat16)
        products = weight_plane.astype(jnp.float32) * warped.astype(jnp.float32)
        target = (dest_block[:, 0] * SLOTS + slot_block).astype(jnp.int32)
        numerator = numerator.at[target].add(products)
        weight_sum = weight_sum.at[target].add(weight_plane.astype(jnp.float32))
        return (numerator, weight_sum), None

    zeros_init = jnp.zeros((N_SKY * SLOTS, TR, TC), jnp.float32)
    (numerator, weight_sum), _ = lax.scan(accumulate, (zeros_init, zeros_init), grouped)
    coadd = numerator / jnp.maximum(weight_sum, 1.0)
    return coadd.reshape(N_SKY * SLOTS * TR, TC)
```

```python
import functools

import jax
import jax.numpy as jnp
from jax import lax
from jax.experimental import pallas as pl
from jax.experimental.pallas import tpu as pltpu
from jax.sharding import PartitionSpec as P

SLOTS = 16
META = 16
GROUP = 16
MESH = pl.DeviceIdType.MESH
VMEM_BYTES = 48 * 1024 * 1024


def toeplitz(basis_vals, distance):
    kernel_len = basis_vals.shape[1]
    picks = (distance[:, :, None] == jnp.arange(kernel_len, dtype=jnp.int32)[None, None, :]).astype(
        jnp.float32
    )
    return jnp.einsum("xyk,bk->bxy", picks, basis_vals.astype(jnp.float32))


def build_tables(basis_rows, basis_cols, tile_rows, tile_cols):
    kernel_len = basis_rows.shape[1]
    out_rows = jnp.arange(tile_rows, dtype=jnp.int32)
    in_rows = jnp.arange(tile_rows + kernel_len - 1, dtype=jnp.int32)
    out_cols = jnp.arange(tile_cols, dtype=jnp.int32)
    in_cols = jnp.arange(2 * tile_cols, dtype=jnp.int32)
    row_table = toeplitz(basis_rows, in_rows[None, :] - out_rows[:, None])
    col_table = toeplitz(basis_cols, in_cols[:, None] - out_cols[None, :])
    return row_table.reshape(-1, row_table.shape[2]), col_table.astype(jnp.bfloat16).reshape(
        -1, tile_cols
    )


def band(taps, shift, length):
    count = taps.shape[0]
    width = taps.shape[1]
    source = lax.broadcasted_iota(jnp.int32, (length, width), 0)
    position = lax.broadcasted_iota(jnp.int32, (length, width), 1)
    offset = source - jnp.clip(position + (shift - count // 2), 0, length - count)
    matrix = jnp.zeros((length, width), jnp.float32)
    for k in range(count):
        matrix = jnp.where(offset == k, taps[k : k + 1, :], matrix)
    return matrix.astype(jnp.bfloat16)


def tiles_kernel(
    capacity,
    tiles,
    coefs,
    row_taps,
    col_taps,
    shifts,
    words,
    weights,
    dest,
    slots,
    row_table,
    col_table,
    send,
    left,
    right,
    scaled,
    prod,
    meta,
    index,
    count,
):
    tile_count = tiles.shape[0]
    basis_count = coefs.shape[1]
    tile_rows = row_taps.shape[2]
    tile_cols = col_taps.shape[2]
    in_rows = row_table.shape[1]
    in_cols = tiles.shape[1] // in_rows
    owners = send.shape[0]
    blocks = tiles.shape[1] // 128

    def clear_index(p, carry):
        index[p] = tile_count
        return carry

    def clear_count(p, carry):
        count[p] = 0
        return carry

    lax.fori_loop(0, owners * capacity, clear_index, 0)
    lax.fori_loop(0, owners, clear_count, 0)

    def place(t, carry):
        owner = dest[t, 0]
        rank = count[owner]
        index[owner * capacity + rank] = t
        count[owner] = rank + 1
        return carry

    lax.fori_loop(0, tile_count, place, 0)
    lane = lax.broadcasted_iota(jnp.int32, (1, 128), 1)
    cell = (lax.broadcasted_iota(jnp.int32, (tile_rows, tile_cols), 0) // (tile_rows // 4)) * 8 + (
        lax.broadcasted_iota(jnp.int32, (tile_rows, tile_cols), 1) // (tile_cols // 8)
    )
    prod[tile_count] = jnp.zeros((tile_rows, tile_cols), jnp.float32)
    meta[tile_count] = jnp.where(lane == 32, 2.0 * SLOTS, jnp.zeros((1, 128), jnp.float32))

    def group(g, carry):
        first = pl.multiple_of(g * GROUP, GROUP)
        for r in range(in_rows):
            a, off = (in_cols * r) // 128, (in_cols * r) % 128
            z = min(a + 3, blocks)
            part = tiles[pl.ds(first, GROUP), a * 128 : z * 128].astype(jnp.float32)
            if off:
                part = pltpu.roll(part, (z - a) * 128 - off, 1)
            left[pl.ds(r, GROUP, stride=in_rows), :] = part[:, :128]
            right[pl.ds(r, GROUP, stride=in_rows), :] = part[:, 128:256]

        def pair(p, inner):
            passes = []
            for half in range(2):
                t = first + 2 * p + half
                base = pl.multiple_of((2 * p + half) * in_rows, in_rows)
                image = jnp.concatenate(
                    [left[pl.ds(base, in_rows), :], right[pl.ds(base, in_rows), :]], axis=1
                ).astype(jnp.bfloat16)
                factors = jnp.concatenate(
                    [
                        row_table[b * tile_rows : (b + 1) * tile_rows, :] * coefs[t, b]
                        for b in range(basis_count)
                    ],
                    axis=0,
                ).astype(jnp.bfloat16)
                passes.append(jnp.dot(factors, image, preferred_element_type=jnp.float32))
            rows = pl.ds(pl.multiple_of(p * 2 * tile_rows, 2 * tile_rows), 2 * tile_rows)
            for b in range(basis_count):
                both = jnp.concatenate(
                    [x[b * tile_rows : (b + 1) * tile_rows, :] for x in passes], axis=0
                )
                scaled[rows, b * 256 : (b + 1) * 256] = both.astype(jnp.bfloat16)
            return inner

        lax.fori_loop(0, GROUP // 2, pair, 0, unroll=2)
        matched = jnp.dot(scaled[...], col_table[...], preferred_element_type=jnp.float32)
        for u in range(GROUP):
            t = first + u
            own = matched[u * tile_rows : (u + 1) * tile_rows, :].astype(jnp.bfloat16)
            row_warp = band(row_taps[t].astype(jnp.float32), shifts[t, 0], tile_rows)
            col_warp = band(col_taps[t].astype(jnp.float32), shifts[t, 1], tile_cols)
            halfway = lax.dot_general(
                row_warp, own, (((0,), (0,)), ((), ())), preferred_element_type=jnp.float32
            ).astype(jnp.bfloat16)
            warped = jnp.dot(halfway, col_warp, preferred_element_type=jnp.float32)
            word, weight = words[t], weights[t]
            good = jnp.bitwise_and(jnp.right_shift(word, cell), 1) == 0
            prod[t] = jnp.where(good, warped * weight, 0.0)
            fine = jnp.bitwise_and(jnp.right_shift(word, jnp.minimum(lane, 31)), 1) == 0
            cells = jnp.where((lane < 32) & fine, weight, 0.0)
            meta[t] = jnp.where(lane == 32, slots[t].astype(jnp.float32), cells)
        return carry

    lax.fori_loop(0, tile_count // GROUP, group, 0)

    def dispatch(owner, carry):
        picks = [index[owner * capacity + r] for r in range(capacity)]
        for r in range(0, capacity, 2):
            both = jnp.concatenate([prod[picks[r]], prod[picks[r + 1]]], axis=0)
            send[owner, r * tile_rows : (r + 2) * tile_rows, :] = both.astype(jnp.bfloat16)
        rows = [meta[k] for k in picks]
        rows.append(jnp.zeros((META - capacity, 128), jnp.float32))
        send[owner, capacity * tile_rows :, :] = jnp.concatenate(rows, axis=0).astype(jnp.bfloat16)
        return carry

    lax.fori_loop(0, owners, dispatch, 0)


def stack_kernel(
    sky, exp, capacity, tile_rows, send, out, held, part, part_held, own_sem, sky_send, sky_recv,
    exp_send, exp_recv
):
    me = lax.axis_index("sky")
    mine = lax.axis_index("exp")
    chunk = send.shape[1]
    share = SLOTS // exp
    body_rows = share * tile_rows
    barrier = pltpu.get_barrier_semaphore()
    for k in range(1, sky):
        pl.semaphore_signal(
            barrier, inc=1, device_id=(lax.rem(me + k, sky), mine), device_id_type=MESH
        )
    for k in range(1, exp):
        pl.semaphore_signal(
            barrier, inc=1, device_id=(me, lax.rem(mine + k, exp)), device_id_type=MESH
        )
    pl.semaphore_wait(barrier, sky + exp - 2)
    copies = []
    order = sorted(range(1, sky), key=lambda k: -min(k, sky - k))
    for k in order:
        owner = lax.rem(me + k, sky)
        copy = pltpu.make_async_remote_copy(
            src_ref=send.at[owner],
            dst_ref=held.at[k],
            send_sem=sky_send.at[k],
            recv_sem=sky_recv.at[k],
            device_id=(owner, mine),
            device_id_type=MESH,
        )
        copy.start()
        copies.append(copy)
    local = pltpu.make_async_copy(send.at[me], held.at[0], own_sem)
    local.start()
    total = sky * chunk
    place = lax.broadcasted_iota(jnp.int32, (1, total), 1)
    source = place // chunk
    within = place - source * chunk
    used = within < capacity * tile_rows
    rank = within // tile_rows
    pixel_row = (within - rank * tile_rows).astype(jnp.float32)
    label = jnp.where(used, source * 8 + rank, -1)
    spread = jnp.where(
        lax.broadcasted_iota(jnp.int32, (sky * 8, total), 0) == label, 1.0, 0.0
    ).astype(jnp.bfloat16)
    local.wait()
    for copy in copies:
        copy.wait()
    info = jnp.concatenate(
        [held[k, capacity * tile_rows :, :].astype(jnp.float32)[:8] for k in range(sky)], axis=0
    )
    which = lax.broadcasted_iota(jnp.int32, (8, sky * 8), 1) % 8
    slot_row = jnp.where(which < capacity, info.T[32:40, :], 2.0 * SLOTS)
    lane_slot = jnp.dot(
        slot_row.astype(jnp.bfloat16), spread, preferred_element_type=jnp.float32
    )[0:1, :]
    goal = jnp.where(used, lane_slot * tile_rows + pixel_row, -1.0)
    out_row = lax.broadcasted_iota(jnp.int32, (SLOTS * tile_rows, total), 0).astype(jnp.float32)
    pick = jnp.where(out_row == goal, 1.0, 0.0).astype(jnp.bfloat16)
    numerator = jnp.dot(
        pick, held[...].reshape(total, held.shape[2]), preferred_element_type=jnp.float32
    )
    slot_pick = jnp.where(
        lax.broadcasted_iota(jnp.int32, (SLOTS, sky * 8), 0).astype(jnp.float32)
        == slot_row[0:1, :],
        1.0,
        0.0,
    ).astype(jnp.bfloat16)
    sums = jnp.dot(slot_pick, info.astype(jnp.bfloat16), preferred_element_type=jnp.float32)
    pad = jnp.zeros((META - share, 128), jnp.float32)
    for e in range(exp):
        part[e, :body_rows, :] = numerator[e * body_rows : (e + 1) * body_rows, :].astype(
            jnp.bfloat16
        )
        part[e, body_rows:, :] = jnp.concatenate(
            [sums[e * share : (e + 1) * share, :], pad], axis=0
        ).astype(jnp.bfloat16)
    swaps = []
    for k in range(1, exp):
        other = lax.rem(mine + k, exp)
        swap = pltpu.make_async_remote_copy(
            src_ref=part.at[other],
            dst_ref=part_held.at[k - 1],
            send_sem=exp_send.at[k - 1],
            recv_sem=exp_recv.at[k - 1],
            device_id=(me, other),
            device_id_type=MESH,
        )
        swap.start()
        swaps.append(swap)
    whole = part[mine].astype(jnp.float32)
    for k, swap in enumerate(swaps):
        swap.wait()
        whole = whole + part_held[k].astype(jnp.float32)
    weight = whole[body_rows : body_rows + share, :]
    columns = out.shape[1]
    cell = lax.broadcasted_iota(jnp.int32, (128, 4 * columns), 0)
    target = lax.broadcasted_iota(jnp.int32, (128, 4 * columns), 1) // (columns // 8)
    widen = jnp.where(cell == target, 1.0, 0.0).astype(jnp.bfloat16)
    high = weight.astype(jnp.bfloat16)
    low = (weight - high.astype(jnp.float32)).astype(jnp.bfloat16)
    wide = jnp.dot(high, widen, preferred_element_type=jnp.float32) + jnp.dot(
        low, widen, preferred_element_type=jnp.float32
    )
    quarter = lax.broadcasted_iota(jnp.int32, (tile_rows, columns), 0) // (tile_rows // 4)
    for q in range(share):
        plane = jnp.zeros((tile_rows, columns), jnp.float32)
        for g in range(4):
            plane = jnp.where(quarter == g, wide[q : q + 1, g * columns : (g + 1) * columns], plane)
        rows = slice(q * tile_rows, (q + 1) * tile_rows)
        out[rows, :] = whole[rows, :] / jnp.maximum(plane, 1.0)


def body(
    padded_tiles,
    coefficients,
    row_taps,
    col_taps,
    shifts,
    mask_words,
    weights,
    destination,
    patch_slot,
    basis_rows,
    basis_cols,
):
    sky = lax.axis_size("sky")
    exp = lax.axis_size("exp")
    tile_count = padded_tiles.shape[0]
    tile_rows = row_taps.shape[2]
    tile_cols = col_taps.shape[2]
    basis_count, kernel_len = basis_rows.shape
    in_rows = tile_rows + kernel_len - 1
    capacity = 2 * ((tile_count + sky - 1) // sky)
    chunk = capacity * tile_rows + META
    row_table, col_table = build_tables(basis_rows, basis_cols, tile_rows, tile_cols)
    vmem = pl.BlockSpec(memory_space=pltpu.VMEM)
    smem = pl.BlockSpec(memory_space=pltpu.SMEM)
    send = pl.pallas_call(
        functools.partial(tiles_kernel, capacity),
        out_shape=jax.ShapeDtypeStruct((sky, chunk, tile_cols), jnp.bfloat16),
        in_specs=[vmem, smem, vmem, vmem, smem, smem, smem, smem, smem, vmem, vmem],
        out_specs=vmem,
        scratch_shapes=[
            pltpu.VMEM((GROUP * in_rows, 128), jnp.float32),
            pltpu.VMEM((GROUP * in_rows, 128), jnp.float32),
            pltpu.VMEM((GROUP * tile_rows, basis_count * 256), jnp.bfloat16),
            pltpu.VMEM((tile_count + 1, tile_rows, tile_cols), jnp.float32),
            pltpu.VMEM((tile_count + 1, 1, 128), jnp.float32),
            pltpu.SMEM((sky * capacity,), jnp.int32),
            pltpu.SMEM((sky,), jnp.int32),
        ],
        compiler_params=pltpu.CompilerParams(vmem_limit_bytes=VMEM_BYTES),
        name="tiles",
    )(
        padded_tiles,
        coefficients,
        row_taps,
        col_taps,
        shifts,
        mask_words,
        weights.astype(jnp.float32),
        destination,
        patch_slot,
        row_table,
        col_table,
    )
    share_rows = SLOTS // exp * tile_rows
    return pl.pallas_call(
        functools.partial(stack_kernel, sky, exp, capacity, tile_rows),
        out_shape=jax.ShapeDtypeStruct((share_rows, tile_cols), jnp.float32),
        in_specs=[vmem],
        out_specs=vmem,
        scratch_shapes=[
            pltpu.VMEM((sky, chunk, tile_cols), jnp.bfloat16),
            pltpu.VMEM((exp, share_rows + META, tile_cols), jnp.bfloat16),
            pltpu.VMEM((max(exp - 1, 1), share_rows + META, tile_cols), jnp.bfloat16),
            pltpu.SemaphoreType.DMA,
            pltpu.SemaphoreType.DMA((sky,)),
            pltpu.SemaphoreType.DMA((sky,)),
            pltpu.SemaphoreType.DMA((max(exp - 1, 1),)),
            pltpu.SemaphoreType.DMA((max(exp - 1, 1),)),
        ],
        compiler_params=pltpu.CompilerParams(
            collective_id=0, has_side_effects=True, vmem_limit_bytes=VMEM_BYTES
        ),
        name="stack",
    )(send)


def solution(mesh):
    placed = (
        P(("sky", "exp"), None),
        P(("sky", "exp"), None),
        P(("sky", "exp"), None, None),
        P(("sky", "exp"), None, None),
        P(("sky", "exp"), None),
        P(("sky", "exp")),
        P(("sky", "exp")),
        P(("sky", "exp"), None),
        P(("sky", "exp")),
        P(),
        P(),
    )
    return jax.shard_map(
        body, mesh=mesh, in_specs=placed, out_specs=P(("sky", "exp"), None), check_vma=False
    )
```

```python
import functools

import jax
import jax.numpy as jnp
from jax import lax
from jax.experimental import pallas as pl
from jax.experimental.pallas import tpu as pltpu
from jax.sharding import PartitionSpec as P

SLOTS = 16
META = 16
GROUP = 16
MESH = pl.DeviceIdType.MESH
VMEM_BYTES = 48 * 1024 * 1024


def plan_kernel(
    sky, capacity, me, dest, rows, cols, plan, row_table, col_table
):
    count = dest.shape[1]
    basis_count = rows.shape[0]
    tile_rows = row_table.shape[0] // basis_count
    tile_cols = col_table.shape[1]
    lane = lax.broadcasted_iota(jnp.int32, (128, 128), 1)
    line = lax.broadcasted_iota(jnp.int32, (128, 128), 0)
    visit = sky - 1 - jnp.bitwise_xor(dest[...], me[0])
    visit = jnp.concatenate([visit, jnp.full((1, 128 - count), sky, jnp.int32)], axis=1)
    visit_across = jnp.broadcast_to(visit, (128, 128))
    visit_down = visit_across.astype(jnp.float32).T.astype(jnp.int32)
    ahead = (visit_down < visit_across) | ((visit_down == visit_across) & (line < lane))
    position = jnp.sum(ahead.astype(jnp.float32), axis=0, keepdims=True)
    position_down = jnp.broadcast_to(position, (128, 128)).T.astype(jnp.int32)
    order = jnp.sum(jnp.where(position_down == lane, line, 0).astype(jnp.float32), axis=0, keepdims=True)
    chunk, rank = lane // capacity, lane % capacity
    start = jnp.sum((visit_down < chunk).astype(jnp.float32), axis=0, keepdims=True)
    held = jnp.sum((visit_down == chunk).astype(jnp.float32), axis=0, keepdims=True)
    rank = rank[0:1, :].astype(jnp.float32)
    place = jnp.where(rank < held, start + rank, float(count))
    plan[...] = jnp.concatenate(
        [order, place, jnp.zeros((6, 128), jnp.float32)], axis=0
    ).astype(jnp.int32)
    for b in range(basis_count):
        row = jnp.broadcast_to(rows[b : b + 1, :], (tile_rows, 128))
        row_table[b * tile_rows : (b + 1) * tile_rows, :] = pltpu.roll(
            row, 0, 1, stride=1, stride_axis=0
        )
        col = jnp.broadcast_to(cols[b : b + 1, :], (128, 128))
        col = pltpu.roll(col, 0, 1, stride=1, stride_axis=0)
        col_table[b * 256 : b * 256 + 128, :] = jnp.where(line >= lane, col, 0.0).astype(jnp.bfloat16)
        col_table[b * 256 + 128 : (b + 1) * 256, :] = jnp.where(line < lane, col, 0.0).astype(
            jnp.bfloat16
        )


def band(taps, shift, length):
    count = taps.shape[0]
    width = taps.shape[1]
    source = lax.broadcasted_iota(jnp.int32, (length, width), 0)
    position = lax.broadcasted_iota(jnp.int32, (length, width), 1)
    offset = source - jnp.clip(position + (shift - count // 2), 0, length - count)
    matrix = jnp.zeros((length, width), jnp.float32)
    for k in range(count):
        matrix = jnp.where(offset == k, taps[k : k + 1, :], matrix)
    return matrix.astype(jnp.bfloat16)


def peer(me, m):
    bit, other = 1, me
    while bit <= m:
        if m & bit:
            other = other + bit * (1 - 2 * lax.rem(me // bit, 2))
        bit *= 2
    return other


def stack_kernel(
    sky,
    exp,
    capacity,
    tiles,
    coefs,
    row_taps,
    col_taps,
    shifts,
    words,
    weights,
    slots,
    plan,
    row_table,
    col_table,
    out,
    left,
    right,
    images,
    scaled,
    prod,
    meta,
    send,
    held,
    part,
    part_held,
    sky_send,
    sky_recv,
    exp_send,
    exp_recv,
):
    me = lax.axis_index("sky")
    mine = lax.axis_index("exp")
    barrier = pltpu.get_barrier_semaphore()
    for m in range(1, sky):
        pl.semaphore_signal(barrier, inc=1, device_id=(peer(me, m), mine), device_id_type=MESH)
    for k in range(1, exp):
        pl.semaphore_signal(
            barrier, inc=1, device_id=(me, lax.rem(mine + k, exp)), device_id_type=MESH
        )
    tile_count = tiles.shape[0]
    basis_count = coefs.shape[0]
    tile_rows = row_taps.shape[2]
    tile_cols = col_taps.shape[2]
    in_rows = images.shape[1]
    in_cols = tiles.shape[1] // in_rows
    blocks = tiles.shape[1] // 128
    chunk = held.shape[1]
    share = SLOTS // exp
    body_rows = share * tile_rows
    lane = lax.broadcasted_iota(jnp.int32, (1, 128), 1)
    cell = (lax.broadcasted_iota(jnp.int32, (tile_rows, tile_cols), 0) // (tile_rows // 4)) * 8 + (
        lax.broadcasted_iota(jnp.int32, (tile_rows, tile_cols), 1) // (tile_cols // 8)
    )
    prod[tile_count] = jnp.zeros((tile_rows, tile_cols), jnp.float32)
    meta[tile_count] = jnp.where(lane == 32, 2.0 * SLOTS, jnp.zeros((1, 128), jnp.float32))

    def unfold(g, carry):
        first = pl.multiple_of(g * GROUP, GROUP)
        for r in range(in_rows):
            a, off = (in_cols * r) // 128, (in_cols * r) % 128
            z = min(a + 3, blocks)
            part_row = tiles[pl.ds(first, GROUP), a * 128 : z * 128].astype(jnp.float32)
            if off:
                part_row = pltpu.roll(part_row, (z - a) * 128 - off, 1)
            left[pl.ds(r, GROUP, stride=in_rows), :] = part_row[:, :128]
            right[pl.ds(r, GROUP, stride=in_rows), :] = part_row[:, 128:256]
        for u in range(GROUP):
            rows = slice(u * in_rows, (u + 1) * in_rows)
            images[first + u] = jnp.concatenate([left[rows, :], right[rows, :]], axis=1).astype(
                jnp.bfloat16
            )
        return carry

    lax.fori_loop(0, tile_count // GROUP, unfold, 0)
    copies, done = [], 0
    for g in range(tile_count // GROUP):
        first = g * GROUP

        def pair(p, inner, first=first):
            passes = []
            for half in range(2):
                t = plan[0, first + 2 * p + half]
                factors = jnp.concatenate(
                    [
                        row_table[b * tile_rows : (b + 1) * tile_rows, :in_rows] * coefs[b, t]
                        for b in range(basis_count)
                    ],
                    axis=0,
                ).astype(jnp.bfloat16)
                passes.append(jnp.dot(factors, images[t], preferred_element_type=jnp.float32))
            rows = pl.ds(pl.multiple_of(p * 2 * tile_rows, 2 * tile_rows), 2 * tile_rows)
            for b in range(basis_count):
                both = jnp.concatenate(
                    [x[b * tile_rows : (b + 1) * tile_rows, :] for x in passes], axis=0
                )
                scaled[rows, b * 256 : (b + 1) * 256] = both.astype(jnp.bfloat16)
            return inner

        lax.fori_loop(0, GROUP // 2, pair, 0, unroll=2)
        matched = jnp.dot(scaled[...], col_table[...], preferred_element_type=jnp.float32)
        for u in range(GROUP):
            t = plan[0, first + u]
            own = matched[u * tile_rows : (u + 1) * tile_rows, :].astype(jnp.bfloat16)
            row_warp = band(row_taps[t].astype(jnp.float32), shifts[0, t], tile_rows)
            col_warp = band(col_taps[t].astype(jnp.float32), shifts[1, t], tile_cols)
            halfway = lax.dot_general(
                row_warp, own, (((0,), (0,)), ((), ())), preferred_element_type=jnp.float32
            ).astype(jnp.bfloat16)
            warped = jnp.dot(halfway, col_warp, preferred_element_type=jnp.float32)
            word, weight = words[t], weights[t]
            good = jnp.bitwise_and(jnp.right_shift(word, cell), 1) == 0
            prod[first + u] = jnp.where(good, warped * weight, 0.0)
            fine = jnp.bitwise_and(jnp.right_shift(word, jnp.minimum(lane, 31)), 1) == 0
            cells = jnp.where((lane < 32) & fine, weight, 0.0)
            meta[first + u] = jnp.where(lane == 32, slots[t].astype(jnp.float32), cells)
        if g == 0:
            pl.semaphore_wait(barrier, sky + exp - 2)
        finished = first + GROUP
        ready = sky if finished == tile_count else min(sky, finished // capacity)
        for v in range(done, ready):
            target = held if v == sky - 1 else send
            picks = [plan[1, v * capacity + r] for r in range(capacity)]
            for r in range(0, capacity, 2):
                both = jnp.concatenate([prod[picks[r]], prod[picks[r + 1]]], axis=0)
                target[v, r * tile_rows : (r + 2) * tile_rows, :] = both.astype(jnp.bfloat16)
            rows = [meta[k] for k in picks]
            rows.append(jnp.zeros((META - capacity, 128), jnp.float32))
            target[v, capacity * tile_rows :, :] = jnp.concatenate(rows, axis=0).astype(
                jnp.bfloat16
            )
            if v < sky - 1:
                copy = pltpu.make_async_remote_copy(
                    src_ref=send.at[v],
                    dst_ref=held.at[v],
                    send_sem=sky_send.at[v],
                    recv_sem=sky_recv.at[v],
                    device_id=(peer(me, sky - 1 - v), mine),
                    device_id_type=MESH,
                )
                copy.start()
                copies.append(copy)
        done = ready
    half = sky // 2
    total = half * chunk
    place = lax.broadcasted_iota(jnp.int32, (1, total), 1)
    source = place // chunk
    within = place - source * chunk
    used = within < capacity * tile_rows
    rank = within // tile_rows
    pixel_row = (within - rank * tile_rows).astype(jnp.float32)
    label = jnp.where(used, source * 8 + rank, -1)
    spread = jnp.where(
        lax.broadcasted_iota(jnp.int32, (half * 8, total), 0) == label, 1.0, 0.0
    ).astype(jnp.bfloat16)
    out_row = lax.broadcasted_iota(jnp.int32, (SLOTS * tile_rows, total), 0).astype(jnp.float32)
    slot_of = lax.broadcasted_iota(jnp.int32, (SLOTS, half * 8), 0).astype(jnp.float32)
    which = lax.broadcasted_iota(jnp.int32, (8, half * 8), 1) % 8
    numerator = sums = None
    for h in range(2):
        for copy in copies[h * half : (h + 1) * half]:
            copy.wait()
        span = range(h * half, (h + 1) * half)
        info = jnp.concatenate(
            [held[k, capacity * tile_rows :, :].astype(jnp.float32)[:8] for k in span], axis=0
        )
        slot_row = jnp.where(which < capacity, info.T[32:40, :], 2.0 * SLOTS)
        lane_slot = jnp.dot(
            slot_row.astype(jnp.bfloat16), spread, preferred_element_type=jnp.float32
        )[0:1, :]
        goal = jnp.where(used, lane_slot * tile_rows + pixel_row, -1.0)
        pick = jnp.where(out_row == goal, 1.0, 0.0).astype(jnp.bfloat16)
        block = held[h * half : (h + 1) * half].reshape(total, held.shape[2])
        more = jnp.dot(pick, block, preferred_element_type=jnp.float32)
        slot_pick = jnp.where(slot_of == slot_row[0:1, :], 1.0, 0.0).astype(jnp.bfloat16)
        extra = jnp.dot(slot_pick, info.astype(jnp.bfloat16), preferred_element_type=jnp.float32)
        numerator = more if h == 0 else numerator + more
        sums = extra if h == 0 else sums + extra
    pad = jnp.zeros((META - share, 128), jnp.float32)
    for e in range(exp):
        part[e, :body_rows, :] = numerator[e * body_rows : (e + 1) * body_rows, :].astype(
            jnp.bfloat16
        )
        part[e, body_rows:, :] = jnp.concatenate(
            [sums[e * share : (e + 1) * share, :], pad], axis=0
        ).astype(jnp.bfloat16)
    swaps = []
    for k in range(1, exp):
        other = lax.rem(mine + k, exp)
        swap = pltpu.make_async_remote_copy(
            src_ref=part.at[other],
            dst_ref=part_held.at[k - 1],
            send_sem=exp_send.at[k - 1],
            recv_sem=exp_recv.at[k - 1],
            device_id=(me, other),
            device_id_type=MESH,
        )
        swap.start()
        swaps.append(swap)
    whole = part[mine].astype(jnp.float32)
    for k, swap in enumerate(swaps):
        swap.wait()
        whole = whole + part_held[k].astype(jnp.float32)
    weight = whole[body_rows : body_rows + share, :]
    columns = out.shape[1]
    cell = lax.broadcasted_iota(jnp.int32, (128, 4 * columns), 0)
    target = lax.broadcasted_iota(jnp.int32, (128, 4 * columns), 1) // (columns // 8)
    widen = jnp.where(cell == target, 1.0, 0.0).astype(jnp.bfloat16)
    high = weight.astype(jnp.bfloat16)
    low = (weight - high.astype(jnp.float32)).astype(jnp.bfloat16)
    wide = jnp.dot(high, widen, preferred_element_type=jnp.float32) + jnp.dot(
        low, widen, preferred_element_type=jnp.float32
    )
    quarter = lax.broadcasted_iota(jnp.int32, (tile_rows, columns), 0) // (tile_rows // 4)
    for q in range(share):
        plane = jnp.zeros((tile_rows, columns), jnp.float32)
        for g in range(4):
            plane = jnp.where(quarter == g, wide[q : q + 1, g * columns : (g + 1) * columns], plane)
        rows = slice(q * tile_rows, (q + 1) * tile_rows)
        out[rows, :] = whole[rows, :] / jnp.maximum(plane, 1.0)


def body(
    padded_tiles,
    coefficients,
    row_taps,
    col_taps,
    shifts,
    mask_words,
    weights,
    destination,
    patch_slot,
    basis_rows,
    basis_cols,
):
    sky = lax.axis_size("sky")
    exp = lax.axis_size("exp")
    tile_count = padded_tiles.shape[0]
    tile_rows = row_taps.shape[2]
    tile_cols = col_taps.shape[2]
    basis_count, kernel_len = basis_rows.shape
    in_rows = tile_rows + kernel_len - 1
    capacity = 2 * ((tile_count + sky - 1) // sky)
    chunk = capacity * tile_rows + META
    vmem = pl.BlockSpec(memory_space=pltpu.VMEM)
    smem = pl.BlockSpec(memory_space=pltpu.SMEM)
    rows = jnp.pad(basis_rows, ((0, 0), (0, 128 - kernel_len))).astype(jnp.float32)
    cols = jnp.concatenate(
        [
            basis_cols[:, :1],
            jnp.zeros((basis_count, 128 - kernel_len), basis_cols.dtype),
            basis_cols[:, :0:-1],
        ],
        axis=1,
    ).astype(jnp.float32)
    plan, row_table, col_table = pl.pallas_call(
        functools.partial(plan_kernel, sky, capacity),
        out_shape=(
            jax.ShapeDtypeStruct((8, 128), jnp.int32),
            jax.ShapeDtypeStruct((basis_count * tile_rows, 128), jnp.float32),
            jax.ShapeDtypeStruct((basis_count * 256, tile_cols), jnp.bfloat16),
        ),
        in_specs=[smem, vmem, vmem, vmem],
        out_specs=(vmem, vmem, vmem),
        compiler_params=pltpu.CompilerParams(vmem_limit_bytes=VMEM_BYTES),
        name="plan",
    )(lax.axis_index("sky").reshape(1), destination.reshape(1, tile_count), rows, cols)
    share_rows = SLOTS // exp * tile_rows
    return pl.pallas_call(
        functools.partial(stack_kernel, sky, exp, capacity),
        out_shape=jax.ShapeDtypeStruct((share_rows, tile_cols), jnp.float32),
        in_specs=[vmem, smem, vmem, vmem, smem, smem, smem, smem, smem, vmem, vmem],
        out_specs=vmem,
        scratch_shapes=[
            pltpu.VMEM((GROUP * in_rows, 128), jnp.float32),
            pltpu.VMEM((GROUP * in_rows, 128), jnp.float32),
            pltpu.VMEM((tile_count, in_rows, 256), jnp.bfloat16),
            pltpu.VMEM((GROUP * tile_rows, basis_count * 256), jnp.bfloat16),
            pltpu.VMEM((tile_count + 1, tile_rows, tile_cols), jnp.float32),
            pltpu.VMEM((tile_count + 1, 1, 128), jnp.float32),
            pltpu.VMEM((sky - 1, chunk, tile_cols), jnp.bfloat16),
            pltpu.VMEM((sky, chunk, tile_cols), jnp.bfloat16),
            pltpu.VMEM((exp, share_rows + META, tile_cols), jnp.bfloat16),
            pltpu.VMEM((max(exp - 1, 1), share_rows + META, tile_cols), jnp.bfloat16),
            pltpu.SemaphoreType.DMA((sky - 1,)),
            pltpu.SemaphoreType.DMA((sky - 1,)),
            pltpu.SemaphoreType.DMA((max(exp - 1, 1),)),
            pltpu.SemaphoreType.DMA((max(exp - 1, 1),)),
        ],
        compiler_params=pltpu.CompilerParams(
            collective_id=0, has_side_effects=True, vmem_limit_bytes=VMEM_BYTES
        ),
        name="stack",
    )(
        padded_tiles,
        coefficients.T,
        row_taps,
        col_taps,
        shifts.T,
        mask_words,
        weights.astype(jnp.float32),
        patch_slot,
        plan,
        row_table,
        col_table,
    )


def solution(mesh):
    placed = (
        P(("sky", "exp"), None),
        P(("sky", "exp"), None),
        P(("sky", "exp"), None, None),
        P(("sky", "exp"), None, None),
        P(("sky", "exp"), None),
        P(("sky", "exp")),
        P(("sky", "exp")),
        P(("sky", "exp"), None),
        P(("sky", "exp")),
        P(),
        P(),
    )
    return jax.shard_map(
        body, mesh=mesh, in_specs=placed, out_specs=P(("sky", "exp"), None), check_vma=False
    )
```

```python
import functools

import jax
import jax.numpy as jnp
from jax import lax
from jax.experimental import pallas as pl
from jax.experimental.pallas import tpu as pltpu
from jax.sharding import PartitionSpec as P

SLOTS = 16
META = 16
GROUP = 16
MESH = pl.DeviceIdType.MESH
VMEM_BYTES = 63 * 1024 * 1024


def plan_kernel(
    sky,
    capacity,
    me,
    dest,
    weights,
    row_taps,
    col_taps,
    basis_rows,
    basis_cols,
    plan,
    scale,
    row_lines,
    col_lines,
    row_table,
    col_table,
    square,
):
    count = dest.shape[1]
    basis_count, kernel_len = basis_rows.shape
    taps, tile_rows = row_taps.shape[:2]
    tile_cols = col_table.shape[1]
    lane = lax.broadcasted_iota(jnp.int32, (128, 128), 1)
    line = lax.broadcasted_iota(jnp.int32, (128, 128), 0)
    visit = sky - 1 - jnp.bitwise_xor(dest[...], me[0])
    visit = jnp.concatenate([visit, jnp.full((1, 128 - count), sky, jnp.int32)], axis=1)
    visit_across = jnp.broadcast_to(visit, (128, 128))
    visit_down = visit_across.astype(jnp.float32).T.astype(jnp.int32)
    ahead = (visit_down < visit_across) | ((visit_down == visit_across) & (line < lane))
    position = jnp.sum(ahead.astype(jnp.float32), axis=0, keepdims=True)
    position_down = jnp.broadcast_to(position, (128, 128)).T.astype(jnp.int32)
    order = jnp.sum(jnp.where(position_down == lane, line, 0).astype(jnp.float32), axis=0, keepdims=True)
    chunk, rank = lane // capacity, lane % capacity
    start = jnp.sum((visit_down < chunk).astype(jnp.float32), axis=0, keepdims=True)
    held = jnp.sum((visit_down == chunk).astype(jnp.float32), axis=0, keepdims=True)
    rank = rank[0:1, :].astype(jnp.float32)
    place = jnp.where(rank < held, start + rank, float(count))
    plan[...] = jnp.concatenate(
        [order, place, jnp.zeros((6, 128), jnp.float32)], axis=0
    ).astype(jnp.int32)
    square[...] = jnp.zeros((128, 128), jnp.float32)
    square[0:1, :count] = weights[...].astype(jnp.float32)
    scale[...] = square[:8, :]
    for k in range(taps):
        square[:tile_rows, :count] = row_taps[k].astype(jnp.float32)
        row_lines[pl.ds(k, count, stride=8), :] = square[...].T[:count, :]
        col_lines[pl.ds(k, count, stride=8), :] = col_taps[k].astype(jnp.float32)
    square[...] = jnp.zeros((128, 128), jnp.float32)
    square[:basis_count, :kernel_len] = basis_cols[...].astype(jnp.float32)
    turned = jnp.where(line == (128 - lane) % 128, 1.0, 0.0).astype(jnp.bfloat16)
    cols = jnp.dot(
        square[...].astype(jnp.bfloat16), turned, preferred_element_type=jnp.float32
    )
    square[:basis_count, :kernel_len] = basis_rows[...].astype(jnp.float32)
    rows = square[...]
    for b in range(basis_count):
        row = jnp.broadcast_to(rows[b : b + 1, :], (tile_rows, 128))
        row_table[b * tile_rows : (b + 1) * tile_rows, :] = pltpu.roll(
            row, 0, 1, stride=1, stride_axis=0
        )
        col = jnp.broadcast_to(cols[b : b + 1, :], (128, 128))
        col = pltpu.roll(col, 0, 1, stride=1, stride_axis=0)
        col_table[b * 256 : b * 256 + 128, :] = jnp.where(line >= lane, col, 0.0).astype(jnp.bfloat16)
        col_table[b * 256 + 128 : (b + 1) * 256, :] = jnp.where(line < lane, col, 0.0).astype(
            jnp.bfloat16
        )


def band(taps, count, shift, length):
    width = taps.shape[1]
    source = lax.broadcasted_iota(jnp.int32, (length, width), 0)
    position = lax.broadcasted_iota(jnp.int32, (length, width), 1)
    offset = source - jnp.clip(position + (shift - count // 2), 0, length - count)
    matrix = jnp.zeros((length, width), jnp.float32)
    for k in range(count):
        matrix = jnp.where(offset == k, taps[k : k + 1, :], matrix)
    return matrix.astype(jnp.bfloat16)


def peer(me, m):
    bit, other = 1, me
    while bit <= m:
        if m & bit:
            other = other + bit * (1 - 2 * lax.rem(me // bit, 2))
        bit *= 2
    return other


def stack_kernel(
    sky,
    exp,
    capacity,
    taps,
    tile_rows,
    tiles,
    coefs,
    shifts,
    words,
    slots,
    plan,
    scale,
    row_lines,
    col_lines,
    row_table,
    col_table,
    out,
    left,
    right,
    images,
    scaled,
    prod,
    meta,
    send,
    held,
    part,
    part_held,
    sky_send,
    sky_recv,
    exp_send,
    exp_recv,
):
    me = lax.axis_index("sky")
    mine = lax.axis_index("exp")
    barrier = pltpu.get_barrier_semaphore()
    for m in range(1, sky):
        pl.semaphore_signal(barrier, inc=1, device_id=(peer(me, m), mine), device_id_type=MESH)
    for k in range(1, exp):
        pl.semaphore_signal(
            barrier, inc=1, device_id=(me, lax.rem(mine + k, exp)), device_id_type=MESH
        )
    tile_count = tiles.shape[0]
    basis_count = coefs.shape[0]
    tile_cols = col_lines.shape[2]
    in_rows = images.shape[1]
    in_cols = tiles.shape[1] // in_rows
    blocks = tiles.shape[1] // 128
    chunk = held.shape[1]
    share = SLOTS // exp
    body_rows = share * tile_rows
    lane = lax.broadcasted_iota(jnp.int32, (1, 128), 1)
    cell = (lax.broadcasted_iota(jnp.int32, (tile_rows, tile_cols), 0) // (tile_rows // 4)) * 8 + (
        lax.broadcasted_iota(jnp.int32, (tile_rows, tile_cols), 1) // (tile_cols // 8)
    )
    prod[tile_count] = jnp.zeros((tile_rows, tile_cols), jnp.float32)
    meta[tile_count] = jnp.where(lane == 32, 2.0 * SLOTS, jnp.zeros((1, 128), jnp.float32))

    def unfold(g, carry):
        first = pl.multiple_of(g * GROUP, GROUP)
        for r in range(in_rows):
            a, off = (in_cols * r) // 128, (in_cols * r) % 128
            z = min(a + 3, blocks)
            part_row = tiles[pl.ds(first, GROUP), a * 128 : z * 128].astype(jnp.float32)
            if off:
                part_row = pltpu.roll(part_row, (z - a) * 128 - off, 1)
            left[pl.ds(r, GROUP, stride=in_rows), :] = part_row[:, :128]
            right[pl.ds(r, GROUP, stride=in_rows), :] = part_row[:, 128:256]
        for u in range(GROUP):
            rows = slice(u * in_rows, (u + 1) * in_rows)
            images[first + u] = jnp.concatenate([left[rows, :], right[rows, :]], axis=1).astype(
                jnp.bfloat16
            )
        return carry

    lax.fori_loop(0, tile_count // GROUP, unfold, 0)
    copies, done = [], 0
    for g in range(tile_count // GROUP):
        first = g * GROUP

        def pair(p, inner, first=first):
            passes = []
            for half in range(2):
                t = plan[0, first + 2 * p + half]
                factors = jnp.concatenate(
                    [
                        row_table[b * tile_rows : (b + 1) * tile_rows, :in_rows] * coefs[b, t]
                        for b in range(basis_count)
                    ],
                    axis=0,
                ).astype(jnp.bfloat16)
                passes.append(jnp.dot(factors, images[t], preferred_element_type=jnp.float32))
            rows = pl.ds(pl.multiple_of(p * 2 * tile_rows, 2 * tile_rows), 2 * tile_rows)
            for b in range(basis_count):
                both = jnp.concatenate(
                    [x[b * tile_rows : (b + 1) * tile_rows, :] for x in passes], axis=0
                )
                scaled[rows, b * 256 : (b + 1) * 256] = both.astype(jnp.bfloat16)
            return inner

        lax.fori_loop(0, GROUP // 2, pair, 0, unroll=4)
        matched = jnp.dot(scaled[...], col_table[...], preferred_element_type=jnp.float32)
        for u in range(GROUP):
            t = plan[0, first + u]
            own = matched[u * tile_rows : (u + 1) * tile_rows, :].astype(jnp.bfloat16)
            row_warp = band(row_lines[t][:, :tile_rows], taps, shifts[0, t], tile_rows)
            col_warp = band(col_lines[t], taps, shifts[1, t], tile_cols)
            halfway = lax.dot_general(
                row_warp, own, (((0,), (0,)), ((), ())), preferred_element_type=jnp.float32
            ).astype(jnp.bfloat16)
            warped = jnp.dot(halfway, col_warp, preferred_element_type=jnp.float32)
            word, weight = words[t], scale[0, t]
            good = jnp.bitwise_and(jnp.right_shift(word, cell), 1) == 0
            prod[first + u] = jnp.where(good, warped * weight, 0.0)
            fine = jnp.bitwise_and(jnp.right_shift(word, jnp.minimum(lane, 31)), 1) == 0
            cells = jnp.where((lane < 32) & fine, weight, 0.0)
            meta[first + u] = jnp.where(lane == 32, slots[t].astype(jnp.float32), cells)
        if g == 0:
            pl.semaphore_wait(barrier, sky + exp - 2)
        finished = first + GROUP
        ready = sky if finished == tile_count else min(sky, finished // capacity)
        for v in range(done, ready):
            target = held if v == sky - 1 else send
            picks = [plan[1, v * capacity + r] for r in range(capacity)]
            for r in range(0, capacity, 2):
                both = jnp.concatenate([prod[picks[r]], prod[picks[r + 1]]], axis=0)
                target[v, r * tile_rows : (r + 2) * tile_rows, :] = both.astype(jnp.bfloat16)
            rows = [meta[k] for k in picks]
            rows.append(jnp.zeros((META - capacity, 128), jnp.float32))
            target[v, capacity * tile_rows :, :] = jnp.concatenate(rows, axis=0).astype(
                jnp.bfloat16
            )
            if v < sky - 1:
                copy = pltpu.make_async_remote_copy(
                    src_ref=send.at[v],
                    dst_ref=held.at[v],
                    send_sem=sky_send.at[v],
                    recv_sem=sky_recv.at[v],
                    device_id=(peer(me, sky - 1 - v), mine),
                    device_id_type=MESH,
                )
                copy.start()
                copies.append(copy)
        done = ready
    half = sky // 2
    total = half * chunk
    place = lax.broadcasted_iota(jnp.int32, (1, total), 1)
    source = place // chunk
    within = place - source * chunk
    used = within < capacity * tile_rows
    rank = within // tile_rows
    pixel_row = (within - rank * tile_rows).astype(jnp.float32)
    label = jnp.where(used, source * 8 + rank, -1)
    spread = jnp.where(
        lax.broadcasted_iota(jnp.int32, (half * 8, total), 0) == label, 1.0, 0.0
    ).astype(jnp.bfloat16)
    out_row = lax.broadcasted_iota(jnp.int32, (SLOTS * tile_rows, total), 0).astype(jnp.float32)
    slot_of = lax.broadcasted_iota(jnp.int32, (SLOTS, half * 8), 0).astype(jnp.float32)
    which = lax.broadcasted_iota(jnp.int32, (8, half * 8), 1) % 8
    numerator = sums = None
    for h in range(2):
        for copy in copies[h * half : (h + 1) * half]:
            copy.wait()
        span = range(h * half, (h + 1) * half)
        info = jnp.concatenate(
            [held[k, capacity * tile_rows :, :].astype(jnp.float32)[:8] for k in span], axis=0
        )
        slot_row = jnp.where(which < capacity, info.T[32:40, :], 2.0 * SLOTS)
        lane_slot = jnp.dot(
            slot_row.astype(jnp.bfloat16), spread, preferred_element_type=jnp.float32
        )[0:1, :]
        goal = jnp.where(used, lane_slot * tile_rows + pixel_row, -1.0)
        pick = jnp.where(out_row == goal, 1.0, 0.0).astype(jnp.bfloat16)
        block = held[h * half : (h + 1) * half].reshape(total, held.shape[2])
        more = jnp.dot(pick, block, preferred_element_type=jnp.float32)
        slot_pick = jnp.where(slot_of == slot_row[0:1, :], 1.0, 0.0).astype(jnp.bfloat16)
        extra = jnp.dot(slot_pick, info.astype(jnp.bfloat16), preferred_element_type=jnp.float32)
        numerator = more if h == 0 else numerator + more
        sums = extra if h == 0 else sums + extra
    pad = jnp.zeros((META - share, 128), jnp.float32)
    for e in range(exp):
        part[e, :body_rows, :] = numerator[e * body_rows : (e + 1) * body_rows, :].astype(
            jnp.bfloat16
        )
        part[e, body_rows:, :] = jnp.concatenate(
            [sums[e * share : (e + 1) * share, :], pad], axis=0
        ).astype(jnp.bfloat16)
    swaps = []
    for k in range(1, exp):
        other = lax.rem(mine + k, exp)
        swap = pltpu.make_async_remote_copy(
            src_ref=part.at[other],
            dst_ref=part_held.at[k - 1],
            send_sem=exp_send.at[k - 1],
            recv_sem=exp_recv.at[k - 1],
            device_id=(me, other),
            device_id_type=MESH,
        )
        swap.start()
        swaps.append(swap)
    whole = part[mine].astype(jnp.float32)
    for k, swap in enumerate(swaps):
        swap.wait()
        whole = whole + part_held[k].astype(jnp.float32)
    weight = whole[body_rows : body_rows + share, :]
    columns = out.shape[1]
    cell = lax.broadcasted_iota(jnp.int32, (128, 4 * columns), 0)
    target = lax.broadcasted_iota(jnp.int32, (128, 4 * columns), 1) // (columns // 8)
    widen = jnp.where(cell == target, 1.0, 0.0).astype(jnp.bfloat16)
    high = weight.astype(jnp.bfloat16)
    low = (weight - high.astype(jnp.float32)).astype(jnp.bfloat16)
    wide = jnp.dot(high, widen, preferred_element_type=jnp.float32) + jnp.dot(
        low, widen, preferred_element_type=jnp.float32
    )
    quarter = lax.broadcasted_iota(jnp.int32, (tile_rows, columns), 0) // (tile_rows // 4)
    for q in range(share):
        plane = jnp.zeros((tile_rows, columns), jnp.float32)
        for g in range(4):
            plane = jnp.where(quarter == g, wide[q : q + 1, g * columns : (g + 1) * columns], plane)
        rows = slice(q * tile_rows, (q + 1) * tile_rows)
        out[rows, :] = whole[rows, :] / jnp.maximum(plane, 1.0)


def body(
    padded_tiles,
    coefficients,
    row_taps,
    col_taps,
    shifts,
    mask_words,
    weights,
    destination,
    patch_slot,
    basis_rows,
    basis_cols,
):
    sky = lax.axis_size("sky")
    exp = lax.axis_size("exp")
    tile_count = padded_tiles.shape[0]
    tile_rows = row_taps.shape[2]
    tile_cols = col_taps.shape[2]
    basis_count, kernel_len = basis_rows.shape
    in_rows = tile_rows + kernel_len - 1
    capacity = 2 * ((tile_count + sky - 1) // sky)
    chunk = capacity * tile_rows + META
    vmem = pl.BlockSpec(memory_space=pltpu.VMEM)
    smem = pl.BlockSpec(memory_space=pltpu.SMEM)
    taps = row_taps.shape[1]
    plan, scale, row_lines, col_lines, row_table, col_table = pl.pallas_call(
        functools.partial(plan_kernel, sky, capacity),
        out_shape=(
            jax.ShapeDtypeStruct((8, 128), jnp.int32),
            jax.ShapeDtypeStruct((8, 128), jnp.float32),
            jax.ShapeDtypeStruct((tile_count * 8, 128), jnp.float32),
            jax.ShapeDtypeStruct((tile_count * 8, tile_cols), jnp.float32),
            jax.ShapeDtypeStruct((basis_count * tile_rows, 128), jnp.float32),
            jax.ShapeDtypeStruct((basis_count * 256, tile_cols), jnp.bfloat16),
        ),
        in_specs=[smem] + [vmem] * 6,
        out_specs=(vmem,) * 6,
        scratch_shapes=[pltpu.VMEM((128, 128), jnp.float32)],
        compiler_params=pltpu.CompilerParams(vmem_limit_bytes=VMEM_BYTES),
        name="plan",
    )(
        lax.axis_index("sky").reshape(1),
        destination.reshape(1, tile_count),
        weights.reshape(1, tile_count),
        row_taps.transpose(1, 2, 0),
        col_taps.transpose(1, 0, 2),
        basis_rows,
        basis_cols,
    )
    share_rows = SLOTS // exp * tile_rows
    return pl.pallas_call(
        functools.partial(stack_kernel, sky, exp, capacity, taps, tile_rows),
        out_shape=jax.ShapeDtypeStruct((share_rows, tile_cols), jnp.float32),
        in_specs=[vmem] + [smem] * 6 + [vmem] * 4,
        out_specs=vmem,
        scratch_shapes=[
            pltpu.VMEM((GROUP * in_rows, 128), jnp.float32),
            pltpu.VMEM((GROUP * in_rows, 128), jnp.float32),
            pltpu.VMEM((tile_count, in_rows, 256), jnp.bfloat16),
            pltpu.VMEM((GROUP * tile_rows, basis_count * 256), jnp.bfloat16),
            pltpu.VMEM((tile_count + 1, tile_rows, tile_cols), jnp.float32),
            pltpu.VMEM((tile_count + 1, 1, 128), jnp.float32),
            pltpu.VMEM((sky - 1, chunk, tile_cols), jnp.bfloat16),
            pltpu.VMEM((sky, chunk, tile_cols), jnp.bfloat16),
            pltpu.VMEM((exp, share_rows + META, tile_cols), jnp.bfloat16),
            pltpu.VMEM((max(exp - 1, 1), share_rows + META, tile_cols), jnp.bfloat16),
            pltpu.SemaphoreType.DMA((sky - 1,)),
            pltpu.SemaphoreType.DMA((sky - 1,)),
            pltpu.SemaphoreType.DMA((max(exp - 1, 1),)),
            pltpu.SemaphoreType.DMA((max(exp - 1, 1),)),
        ],
        compiler_params=pltpu.CompilerParams(
            collective_id=0, has_side_effects=True, vmem_limit_bytes=VMEM_BYTES
        ),
        name="stack",
    )(
        padded_tiles,
        coefficients.T,
        shifts.T,
        mask_words,
        patch_slot,
        plan,
        scale,
        row_lines.reshape(tile_count, 8, 128),
        col_lines.reshape(tile_count, 8, tile_cols),
        row_table,
        col_table,
    )


def solution(mesh):
    placed = (
        P(("sky", "exp"), None),
        P(("sky", "exp"), None),
        P(("sky", "exp"), None, None),
        P(("sky", "exp"), None, None),
        P(("sky", "exp"), None),
        P(("sky", "exp")),
        P(("sky", "exp")),
        P(("sky", "exp"), None),
        P(("sky", "exp")),
        P(),
        P(),
    )
    return jax.shard_map(
        body, mesh=mesh, in_specs=placed, out_specs=P(("sky", "exp"), None), check_vma=False
    )
```
